32 devices in a mesh: member: 16 (over z, y, core), tensor: 2 (over x).
Axes of the slice: x: 2, y: 2, z: 4, core: 2. Of those that a mesh axis runs over, the one named last changes fastest.
Arguments:
- prompt_states: bfloat16 [8192, 5120], P('member', 'tensor'), may hold values from -6 to 6
- decode_states: bfloat16 [4096, 5120], P('member', 'tensor'), may hold values from -6 to 6
- norm_gain: bfloat16 [5120], P('tensor'), may hold values from 0.5 to 7, as said below
- query_bias: bfloat16 [5120], P('tensor'), may hold values from -3 to 3
- value_bias: bfloat16 [1024], P('tensor'), may hold values from -3 to 3
- w_query: bfloat16 [5120, 5120], P('member', 'tensor'), may hold values from -0.078125 to 0.078125
- w_key: bfloat16 [5120, 1024], P('member', 'tensor'), may hold values from -0.078125 to 0.078125
- w_value: bfloat16 [5120, 1024], P('member', 'tensor'), may hold values from -0.078125 to 0.078125
- w_out: bfloat16 [5120, 5120], P('tensor', 'member'), may hold values from -0.078125 to 0.078125
- targets: bfloat16 [4096, 5120], P('member', 'tensor'), may hold values from -3 to 3
- lengths: int32 [32], replicated, may hold values from 1 to 128, 2048 in all
- seeds: int32 [16], replicated, may hold values from 0 to 46336
Outputs:
- fitness: float32 [32], replicated
- grad_query: float32 [5120, 5120], P('member', 'tensor')
- grad_key: float32 [5120, 1024], P('member', 'tensor')
- grad_value: float32 [5120, 1024], P('member', 'tensor')
- grad_out: float32 [5120, 5120], P('tensor', 'member')
The draws below stay inside these ranges and needn't reach their ends.
Inputs may be any that keep to these rules, and one draw needn't show every extreme that they name: lengths[2 m] and lengths[2 m + 1] belong to pair m; all lengths sum to exactly 2048, and one of them equals 128. `norm_gain`: positive gains.
All inputs are finite; a program needn't handle non-finite values.
Results may differ from the reference program's by a relative error of at most 0.018.
The reference program's roundings to bfloat16 on the way count: a program that leaves them out, or rounds other values in their place, can miss the bound.
Values may be sent and summed in bfloat16 or wider, within the bound.
A program may use at most 192 MiB of HBM per device.

```python
import math
import jax
import jax.numpy as jnp
import numpy as np
from jax import lax

D = 5120
HEADS = 40
KV_HEADS = 8
HEAD_DIM = 128
PROMPT = 512
DEC = 128
RANK = 16
POP = 32
PROMPT_ROWS = 8192
DECODE_ROWS = 4096
N_MEMBER = 16
N_TENSOR = 2


def draw_norm_gain(key, part):
    values = 1.0 + 0.15 * jax.random.normal(key, (D,), jnp.float32)
    return jnp.clip(values, 0.5, 1.5).astype(jnp.bfloat16)


def plant(array, stream_key, smallest, largest):
    longest = array.shape.index(max(array.shape))
    spots = []
    for shift in (0, 1):
        where = [jax.random.randint(jax.random.fold_in(stream_key, axis), (), 0, length) for axis, length in enumerate(array.shape)]
        where[longest] = (where[longest] + shift) % array.shape[longest]
        spots.append(tuple(where))
    return array.at[spots[0]].set(smallest).at[spots[1]].set(largest)


def level_of(own_key, shape, cuts, low, high):
    def one(axis_at, shards_of):
        draws = jax.random.uniform(jax.random.fold_in(jax.random.fold_in(own_key, 6), axis_at), (shards_of,), jnp.float32, low / len(cuts), high / len(cuts))
        return jnp.repeat(jnp.exp(draws), shape[axis_at] // shards_of).reshape((-1,) + (1,) * (len(shape) - axis_at - 1))

    loudness = one(*cuts[0])
    for cut in cuts[1:]:
        loudness = loudness * one(*cut)
    return loudness


def length_profile(number_of, total, reach, lean):
    weights = [(1 << 20) // math.isqrt(grade ** lean) + 1 for grade in range(2, number_of + 1)]
    spare, counts = total - reach - (number_of - 1), [1] * (number_of - 1)
    while spare > 0:
        free = [i for i in range(number_of - 1) if counts[i] < reach]
        pool, budget = sum([weights[i] for i in free]), spare
        for i in free:
            addition = min(reach - counts[i], max(1, budget * weights[i] // pool), spare)
            counts[i] = counts[i] + addition
            spare = spare - addition
    return np.array([reach] + counts)


def uneven(stream_key, number_of, total, most, skew):
    if number_of == 2:
        one = jax.random.randint(stream_key, (), max(1, total - most), min(most, total - 1) + 1)
        return jnp.stack([one, total - one])
    sizes = jnp.asarray(length_profile(number_of, total, most, skew), jnp.int32)
    couples = (number_of - 1) // 2
    donor, sink = sizes[1:1 + 2 * couples:2], sizes[2:2 + 2 * couples:2]
    slack = jnp.minimum(donor - 1, most - sink)
    shifted = jax.random.randint(jax.random.fold_in(stream_key, 1), (couples,), 0, 1 << 20) % (slack + 1)
    sizes = sizes.at[1:1 + 2 * couples:2].set(donor - shifted).at[2:2 + 2 * couples:2].set(sink + shifted)
    return sizes[jax.random.permutation(jax.random.fold_in(stream_key, 2), number_of)]


def centred(rng, dims, deviation, reach, cuts=(), held_as=jnp.bfloat16):
    entries = jax.random.normal(rng, dims, jnp.float32) * deviation
    if len(cuts) > 0:
        entries = level_of(rng, dims, cuts, -0.22, 0.18) * entries
    return jnp.clip(entries, min=-reach, max=reach).astype(held_as)


def setup_inputs(seed: int = 0) -> dict:
    streams_of = jax.random.split(jax.random.key(seed), 13)
    return {
        "prompt_states": centred(streams_of[0], (PROMPT_ROWS, D), 1.0, 6.0, ((0, 16), (1, 2))),
        "decode_states": centred(streams_of[1], (DECODE_ROWS, D), 1.0, 6.0, ((0, 16), (1, 2))),
        "norm_gain": draw_norm_gain(jax.random.fold_in(streams_of[12], 71), 0),
        "query_bias": centred(streams_of[3], (HEADS * HEAD_DIM,), 0.5, 3.0, ((0, 2),)),
        "value_bias": centred(streams_of[4], (KV_HEADS * HEAD_DIM,), 0.5, 3.0, ((0, 2),)),
        "w_query": centred(streams_of[5], (D, HEADS * HEAD_DIM), D ** -0.5, 0.078125, ((0, 16), (1, 2))),
        "w_key": centred(streams_of[6], (D, KV_HEADS * HEAD_DIM), D ** -0.5, 0.078125, ((0, 16), (1, 2))),
        "w_value": centred(streams_of[7], (D, KV_HEADS * HEAD_DIM), D ** -0.5, 0.078125, ((0, 16), (1, 2))),
        "w_out": centred(streams_of[8], (HEADS * HEAD_DIM, D), (HEADS * HEAD_DIM) ** -0.5, 0.078125, ((0, 2), (1, 16))),
        "targets": centred(streams_of[9], (DECODE_ROWS, D), 0.5, 3.0, ((0, 16), (1, 2))),
        "lengths": uneven(streams_of[10], POP, N_MEMBER * DEC, DEC, 2).astype(jnp.int32),
        "seeds": plant(jax.random.randint(streams_of[11], (N_MEMBER,), 0, 46337), jax.random.fold_in(streams_of[11], 1), 0, 46336).astype(jnp.int32),
    }


PRIME = 46337
SIGMA_SCALE = 0.3
NEG_LARGE = -1e+30

def noise_table(seed_value, matrix_id, positions, rank_count):
    rank_ids = jnp.arange(rank_count, dtype=jnp.int32)
    mixing_matrix = (seed_value + (matrix_id * rank_count + rank_ids)[None, :] * 2749 + positions[:, None] * 6271) % PRIME
    hashed = (mixing_matrix * mixing_matrix + 1013) % PRIME
    hashed = (hashed * hashed + mixing_matrix) % PRIME
    hashed = (hashed * hashed + 1013) % PRIME
    return ((hashed.astype(jnp.float32) * (2.0 / PRIME) - 1.0) * math.sqrt(3.0)).astype(jnp.bfloat16)

def normed(states, gain):
    values = states.astype(jnp.float32)
    scale = lax.rsqrt(lax.optimization_barrier(jnp.mean(values * values, axis=-1, keepdims=True)) + 1e-06)
    return (values * scale * gain.astype(jnp.float32)).astype(jnp.bfloat16)

def low_term(left_factor, table_a, table_b):
    inner = jnp.dot(left_factor, table_a, preferred_element_type=jnp.float32)
    return jnp.dot(inner, table_b.astype(jnp.float32).T, precision=lax.Precision.HIGHEST)

def attend(query, keys, values, group, head_dim, prompt_len):
    count = query.shape[0]
    kv_count = keys.shape[1] // head_dim
    query_four = query.astype(jnp.float32).reshape(count, kv_count, group, head_dim)
    keys_three = keys.astype(jnp.float32).reshape(-1, kv_count, head_dim)
    values_three = values.astype(jnp.float32).reshape(-1, kv_count, head_dim)
    scores = jnp.einsum('pkgd,nkd->kgpn', query_four, keys_three) / math.sqrt(head_dim)
    key_index = jnp.arange(keys_three.shape[0], dtype=jnp.int32) - prompt_len
    query_index = jnp.arange(count, dtype=jnp.int32)
    allowed = key_index[None, :] <= query_index[:, None]
    scores = jnp.where(allowed, scores, NEG_LARGE)
    top = lax.optimization_barrier(jnp.max(scores, axis=-1, keepdims=True))
    exponent = jnp.exp(scores - top)
    weights = (exponent / lax.optimization_barrier(jnp.sum(exponent, axis=-1, keepdims=True))).astype(jnp.bfloat16)
    mixed = jnp.einsum('kgpn,nkd->pkgd', weights.astype(jnp.float32), values_three)
    return mixed.astype(jnp.bfloat16).reshape(count, kv_count * group * head_dim)

def reference(prompt_states, decode_states, norm_gain, query_bias, value_bias, w_query, w_key, w_value, w_out, targets, lengths, seeds):
    sigma = SIGMA_SCALE / math.sqrt(D)
    lift = sigma / math.sqrt(RANK)
    group = HEADS // KV_HEADS
    share_width = HEADS * HEAD_DIM // N_TENSOR
    row_ids = jnp.arange(D, dtype=jnp.int32)
    query_cols = jnp.arange(HEADS * HEAD_DIM, dtype=jnp.int32)
    pair_cols = jnp.arange(KV_HEADS * HEAD_DIM, dtype=jnp.int32)

    def member_fitness(member):
        seed_value = seeds[member]
        prompt_rows = lax.dynamic_slice_in_dim(prompt_states, member * PROMPT, PROMPT, 0)
        decode_rows = lax.dynamic_slice_in_dim(decode_states, member * 2 * DEC, 2 * DEC, 0)
        goal = lax.dynamic_slice_in_dim(targets, member * 2 * DEC, 2 * DEC, 0).astype(jnp.float32)
        prompt_normed = normed(prompt_rows, norm_gain)
        decode_normed = normed(decode_rows, norm_gain)
        a_query = noise_table(seed_value, 0, row_ids, RANK)
        a_key = noise_table(seed_value, 1, row_ids, RANK)
        a_value = noise_table(seed_value, 2, row_ids, RANK)
        a_out = noise_table(seed_value, 3, query_cols, RANK)
        b_query = noise_table(seed_value, 4, query_cols, RANK)
        b_key = noise_table(seed_value, 5, pair_cols, RANK)
        b_value = noise_table(seed_value, 6, pair_cols, RANK)
        b_out = noise_table(seed_value, 7, row_ids, RANK)
        prompt_key_base = jnp.dot(prompt_normed, w_key, preferred_element_type=jnp.float32)
        prompt_value_base = jnp.dot(prompt_normed, w_value, preferred_element_type=jnp.float32)
        low_prompt_key = low_term(prompt_normed, a_key, b_key)
        low_prompt_value = low_term(prompt_normed, a_value, b_value)
        query_base = jnp.dot(decode_normed, w_query, preferred_element_type=jnp.float32)
        key_base = jnp.dot(decode_normed, w_key, preferred_element_type=jnp.float32)
        value_base = jnp.dot(decode_normed, w_value, preferred_element_type=jnp.float32)
        low_query = low_term(decode_normed, a_query, b_query)
        low_key = low_term(decode_normed, a_key, b_key)
        low_value = low_term(decode_normed, a_value, b_value)
        results = []
        for sign_index in range(2):
            sign = 1.0 - 2.0 * sign_index
            first = sign_index * DEC
            last = first + DEC
            prompt_key = (prompt_key_base + sign * lift * low_prompt_key).astype(jnp.bfloat16)
            prompt_value = (prompt_value_base + value_bias.astype(jnp.float32) + sign * lift * low_prompt_value).astype(jnp.bfloat16)
            query = (query_base[first:last] + query_bias.astype(jnp.float32) + sign * lift * low_query[first:last]).astype(jnp.bfloat16)
            key = (key_base[first:last] + sign * lift * low_key[first:last]).astype(jnp.bfloat16)
            value = (value_base[first:last] + value_bias.astype(jnp.float32) + sign * lift * low_value[first:last]).astype(jnp.bfloat16)
            mixed = attend(query, jnp.concatenate([prompt_key, key], axis=0), jnp.concatenate([prompt_value, value], axis=0), group, HEAD_DIM, PROMPT)
            output = jnp.zeros((DEC, D), jnp.float32)
            for share in range(N_TENSOR):
                low_col = share * share_width
                high_col = low_col + share_width
                mixed_share = mixed[:, low_col:high_col]
                partial_value = jnp.dot(mixed_share, w_out[low_col:high_col], preferred_element_type=jnp.float32) + sign * lift * low_term(mixed_share, a_out[low_col:high_col], b_out)
                rounded = lax.optimization_barrier(partial_value.astype(jnp.bfloat16))
                output = output + rounded.astype(jnp.float32)
            difference = output - goal[first:last]
            fitness_errors = lax.optimization_barrier(jnp.sum(difference * difference, axis=1)) / D
            length = lengths[2 * member + sign_index]
            live = jnp.arange(DEC, dtype=jnp.int32) < length
            results.append(-jnp.sum(jnp.where(live, fitness_errors, 0.0)) / length.astype(jnp.float32))
        return jnp.stack(results)
    fitness = lax.map(member_fitness, jnp.arange(N_MEMBER, dtype=jnp.int32)).reshape(2 * N_MEMBER)
    differences = fitness[0::2] - fitness[1::2]
    factor = 1.0 / (2.0 * N_MEMBER * sigma * math.sqrt(RANK))
    row_of_weights = differences * factor

    def update(first_id, second_id, left_ids, right_ids):
        left_factor = jax.vmap(lambda seed_one: noise_table(seed_one, first_id, left_ids, RANK))(seeds).astype(jnp.float32)
        right_factor = jax.vmap(lambda seed_one: noise_table(seed_one, second_id, right_ids, RANK))(seeds).astype(jnp.float32)
        return jnp.einsum('lqh,lah->qa', left_factor * row_of_weights[:, None, None], right_factor, precision=lax.Precision.HIGHEST)
    grad_query = update(0, 4, row_ids, query_cols)
    grad_key = update(1, 5, row_ids, pair_cols)
    grad_value = update(2, 6, row_ids, pair_cols)
    grad_out = update(3, 7, query_cols, row_ids)
    return (fitness, grad_query, grad_key, grad_value, grad_out)
```

```python
import math

import jax
import jax.numpy as jnp
from jax import lax
from jax.sharding import PartitionSpec as P

D = 5120
HEADS = 40
KV_HEADS = 8
HEAD_DIM = 128
DEC = 128
RANK = 16


PRIME = 46337
SIGMA_SCALE = 0.3
NEG_LARGE = -1e30


def noise_rows(seed_value, matrix_id, positions):
    rank_ids = jnp.arange(RANK, dtype=jnp.int32)
    mixing = (
        seed_value + (matrix_id * RANK + rank_ids)[:, None] * 2749 + positions[None, :] * 6271
    ) % PRIME
    hashed = (mixing * mixing + 1013) % PRIME
    hashed = (hashed * hashed + mixing) % PRIME
    hashed = (hashed * hashed + 1013) % PRIME
    return ((hashed.astype(jnp.float32) * (2.0 / PRIME) - 1.0) * math.sqrt(3.0)).astype(
        jnp.bfloat16
    )


def normed(states, gain):
    values = states.astype(jnp.float32)
    scale = lax.rsqrt(jnp.mean(values * values, axis=-1, keepdims=True) + 1e-06)
    return (values * scale * gain.astype(jnp.float32)).astype(jnp.bfloat16)


def parts_of(values, count):
    parts = []
    for _ in range(count):
        part = lax.reduce_precision(values, 8, 7)
        parts.append(part.astype(jnp.bfloat16))
        values = values - part
    return parts


def expand(inner, rows_b):
    parts = parts_of(inner, 3)
    return jnp.dot(
        jnp.concatenate(parts, axis=1),
        jnp.concatenate([rows_b] * 3, axis=0),
        preferred_element_type=jnp.float32,
    )


def times_rows(left, rows):
    return lax.dot_general(
        left, rows, (((1,), (1,)), ((), ())), preferred_element_type=jnp.float32
    )


def attend(query, keys, values, group, head_dim, prompt_len):
    count = query.shape[0]
    kv_count = keys.shape[1] // head_dim
    query_four = query.reshape(count, kv_count, group, head_dim)
    keys_three = keys.reshape(-1, kv_count, head_dim)
    values_three = values.reshape(-1, kv_count, head_dim)
    scores = jnp.einsum(
        "pkgd,nkd->kgpn", query_four, keys_three, preferred_element_type=jnp.float32
    ) / math.sqrt(head_dim)
    key_index = jnp.arange(keys_three.shape[0], dtype=jnp.int32) - prompt_len
    query_index = jnp.arange(count, dtype=jnp.int32)
    allowed = key_index[None, :] <= query_index[:, None]
    scores = jnp.where(allowed, scores, NEG_LARGE)
    top = jnp.max(scores, axis=-1, keepdims=True)
    exponent = jnp.exp(scores - top)
    weights = (exponent / jnp.sum(exponent, axis=-1, keepdims=True)).astype(jnp.bfloat16)
    mixed = jnp.einsum("kgpn,nkd->pkgd", weights, values_three, preferred_element_type=jnp.float32)
    return mixed.astype(jnp.bfloat16).reshape(count, kv_count * group * head_dim)


def chip_cycle(chips):
    wide = chips // 4
    walk = [(a, 0) for a in range(4)]
    for a in (3, 2, 1, 0):
        columns = list(range(1, wide))
        if a % 2 == 0:
            columns = columns[::-1]
        walk += [(a, b) for b in columns]
    return [a * wide + b for a, b in walk]


def ring_step(piece, cycle, shift):
    count = len(cycle)
    perm = []
    for place, chip in enumerate(cycle):
        other = cycle[(place + shift) % count]
        perm += [(2 * chip + core, 2 * other + core) for core in range(2)]
    return lax.ppermute(piece, "member", perm)


def to_sibling(piece, members):
    return lax.ppermute(piece, "member", [(m, m ^ 1) for m in range(members)])


def ring_gather(shard, cycle, place, after=None):
    count = len(cycle)
    table = jnp.array(cycle, jnp.int32)
    rows = shard.shape[0]
    half = rows // 2
    if after is not None:
        shard, _ = lax.optimization_barrier((shard, after))
    found = [(table[place], shard)]
    forward = backward = shard
    for step in range(1, count // 2):
        forward = ring_step(forward, cycle, 1)
        backward = ring_step(backward, cycle, -1)
        found.append((table[(place - step) % count], forward))
        found.append((table[(place + step) % count], backward))
    forward = ring_step(forward[:half], cycle, 1)
    backward = ring_step(backward[half:], cycle, -1)
    far = table[(place + count // 2) % count]
    found.append((far, jnp.concatenate([forward, backward], axis=0)))
    return found, (forward, backward)


def per_device(
    prompt_states,
    decode_states,
    norm_gain,
    query_bias,
    value_bias,
    w_query,
    w_key,
    w_value,
    w_out,
    targets,
    lengths,
    seeds,
):
    members = lax.axis_size("member")
    tensors = lax.axis_size("tensor")
    member_id = lax.axis_index("member")
    tensor_id = lax.axis_index("tensor")
    core = member_id % 2
    cycle = chip_cycle(members // 2)
    places = [0] * len(cycle)
    for place_at, chip in enumerate(cycle):
        places[chip] = place_at
    place = jnp.array(places, jnp.int32)[member_id // 2]
    shard_width = prompt_states.shape[1]
    prompt_len = prompt_states.shape[0]
    query_width = w_query.shape[1]
    pair_width = w_key.shape[1]
    piece_rows = w_query.shape[0]
    out_piece = w_out.shape[1]
    group = HEADS // KV_HEADS
    sigma = SIGMA_SCALE / math.sqrt(D)
    lift = sigma / math.sqrt(RANK)
    seed_value = seeds[member_id]
    length_plus = lengths[2 * member_id]
    negative_length = lengths[2 * member_id + 1]
    local_rows = jnp.arange(2 * DEC, dtype=jnp.int32)
    plus_rows = local_rows < DEC
    positions = local_rows % DEC
    row_live = positions < jnp.where(plus_rows, length_plus, negative_length)
    column_signs = jnp.where(plus_rows, 1.0, -1.0).astype(jnp.float32)[:, None]

    in_shard = jnp.concatenate([w_query, w_key, w_value], axis=1)
    out_shard = w_out.T
    lane_rows = piece_rows // 2
    query_all = jnp.zeros((D, query_width), jnp.bfloat16)
    pair_all = jnp.zeros((D, 2 * pair_width), jnp.bfloat16)
    out_lanes = []
    for lane in range(2):
        first = lane * lane_rows
        found, last = ring_gather(in_shard[first : first + lane_rows], cycle, place)
        for chip, piece in found:
            for owner, block in ((core, piece), (1 - core, to_sibling(piece, members))):
                start = (2 * chip + owner) * piece_rows + first
                query_all = lax.dynamic_update_slice_in_dim(
                    query_all, block[:, :query_width], start, 0
                )
                pair_all = lax.dynamic_update_slice_in_dim(
                    pair_all, block[:, query_width:], start, 0
                )
        out_found, _ = ring_gather(out_shard[first : first + lane_rows], cycle, place, last)
        out_lanes.append(out_found)

    prompt_full, decode_full, gain_full = (
        lax.all_gather(prompt_states, "tensor", axis=1, tiled=True),
        lax.all_gather(decode_states, "tensor", axis=1, tiled=True),
        lax.all_gather(norm_gain[None, :], "tensor", axis=1, tiled=True),
    )
    gain_row = gain_full[0]
    all_normed = normed(jnp.concatenate([decode_full, prompt_full], axis=0), gain_row)
    decode_normed = all_normed[: 2 * DEC]
    row_ids = jnp.arange(D, dtype=jnp.int32)
    query_cols = tensor_id * query_width + jnp.arange(query_width, dtype=jnp.int32)
    pair_cols = tensor_id * pair_width + jnp.arange(pair_width, dtype=jnp.int32)
    tables_left = jnp.concatenate([noise_rows(seed_value, g, row_ids) for g in range(3)], axis=0)
    inner = times_rows(all_normed, tables_left)
    low_query = expand(inner[: 2 * DEC, :RANK], noise_rows(seed_value, 4, query_cols))
    low_key = expand(inner[:, RANK : 2 * RANK], noise_rows(seed_value, 5, pair_cols))
    low_value = expand(inner[:, 2 * RANK :], noise_rows(seed_value, 6, pair_cols))
    low_pair = jnp.concatenate([low_key, low_value], axis=1)
    pair_bias = jnp.concatenate(
        [jnp.zeros((pair_width,), jnp.float32), value_bias.astype(jnp.float32)]
    )
    query_base = jnp.dot(decode_normed, query_all, preferred_element_type=jnp.float32)
    pair_base = jnp.dot(all_normed, pair_all, preferred_element_type=jnp.float32)
    query = (query_base + query_bias.astype(jnp.float32) + column_signs * lift * low_query).astype(
        jnp.bfloat16
    )
    pair_base = pair_base + pair_bias
    mixed_parts = []
    for sign_index in range(2):
        sign = 1.0 - 2.0 * sign_index
        first = sign_index * DEC
        last = first + DEC
        own = jnp.concatenate([pair_base[2 * DEC :], pair_base[first:last]], axis=0)
        own_low = jnp.concatenate([low_pair[2 * DEC :], low_pair[first:last]], axis=0)
        pair = (own + sign * lift * own_low).astype(jnp.bfloat16)
        mixed_parts.append(
            attend(
                query[first:last],
                pair[:, :pair_width],
                pair[:, pair_width:],
                group,
                HEAD_DIM,
                prompt_len,
            )
        )
    mixed = jnp.concatenate(mixed_parts, axis=0)
    out_inner = times_rows(mixed, noise_rows(seed_value, 3, query_cols))
    out_low = expand(out_inner, noise_rows(seed_value, 7, row_ids))
    out_low = column_signs * lift * out_low

    summed = jnp.zeros((2 * DEC, D), jnp.float32)
    for (chip, piece_a), (_, piece_b) in zip(*out_lanes):
        near = jnp.concatenate([piece_a, piece_b], axis=0)
        far = to_sibling(near, members)
        low_part = lax.dynamic_slice_in_dim(out_low, chip * 2 * out_piece, 2 * out_piece, 1)
        partial = []
        for block in (near, far):
            partial.append(times_rows(mixed, block))
        both = [
            jnp.where(core == 0, partial[0], partial[1]),
            jnp.where(core == 0, partial[1], partial[0]),
        ]
        chunk = jnp.concatenate(both, axis=1)
        chunk = (chunk + low_part).astype(jnp.bfloat16)
        if tensors == 2:
            other = lax.ppermute(chunk, "tensor", [(0, 1), (1, 0)])
            chunk = chunk.astype(jnp.float32) + other.astype(jnp.float32)
        else:
            chunk = lax.psum(chunk, "tensor").astype(jnp.float32)
        summed = lax.dynamic_update_slice_in_dim(summed, chunk, chip * 2 * out_piece, 1)

    shared = lax.dynamic_slice_in_dim(summed, tensor_id * shard_width, shard_width, 1)
    difference = shared - targets.astype(jnp.float32)
    fitness_errors = jnp.sum(difference * difference, axis=1) / D
    fitness_errors = jnp.where(row_live, fitness_errors, 0.0)
    pair_total = jnp.stack(
        [
            jnp.sum(fitness_errors[:DEC]) / length_plus.astype(jnp.float32),
            jnp.sum(fitness_errors[DEC:]) / negative_length.astype(jnp.float32),
        ]
    )
    spread = lax.dynamic_update_slice_in_dim(
        jnp.zeros((2 * members,), jnp.float32), pair_total, 2 * member_id, 0
    )
    fitness = -lax.psum(spread, ("member", "tensor"))
    differences = fitness[0::2] - fitness[1::2]
    factor = 1.0 / (2.0 * members * sigma * math.sqrt(RANK))
    row_of_weights = differences * factor
    own_rows = member_id * piece_rows + jnp.arange(piece_rows, dtype=jnp.int32)
    own_out_cols = member_id * out_piece + jnp.arange(out_piece, dtype=jnp.int32)

    def all_rows(matrix_id, ids):
        tables = jax.vmap(lambda seed_one: noise_rows(seed_one, matrix_id, ids))(seeds)
        return tables.reshape(members * RANK, ids.shape[0])

    row_weights = jnp.repeat(row_of_weights, RANK)[:, None]

    def update(first_id, second_id, left_ids, right_ids):
        left = all_rows(first_id, left_ids)
        right = all_rows(second_id, right_ids)
        if left_ids.shape[0] <= right_ids.shape[0]:
            left = jnp.concatenate(parts_of(left.astype(jnp.float32) * row_weights, 2), axis=0)
            right = jnp.concatenate([right, right], axis=0)
        else:
            right = jnp.concatenate(parts_of(right.astype(jnp.float32) * row_weights, 2), axis=0)
            left = jnp.concatenate([left, left], axis=0)
        return lax.dot_general(
            left, right, (((0,), (0,)), ((), ())), preferred_element_type=jnp.float32
        )

    grad_query = update(0, 4, own_rows, query_cols)
    grad_key = update(1, 5, own_rows, pair_cols)
    grad_value = update(2, 6, own_rows, pair_cols)
    grad_out = update(3, 7, query_cols, own_out_cols)
    return (fitness, grad_query, grad_key, grad_value, grad_out)


def solution(mesh):
    placed = (
        P("member", "tensor"),
        P("member", "tensor"),
        P("tensor"),
        P("tensor"),
        P("tensor"),
        P("member", "tensor"),
        P("member", "tensor"),
        P("member", "tensor"),
        P("tensor", "member"),
        P("member", "tensor"),
        P(),
        P(),
    )
    return jax.shard_map(
        per_device,
        mesh=mesh,
        in_specs=placed,
        out_specs=(
            P(),
            P("member", "tensor"),
            P("member", "tensor"),
            P("member", "tensor"),
            P("tensor", "member"),
        ),
        check_vma=False,
    )
```

```python
import functools
import math

import jax
import jax.numpy as jnp
from jax import lax
from jax.experimental import pallas as pl
from jax.experimental.pallas import tpu as pltpu
from jax.sharding import PartitionSpec as P

D = 5120
HEADS = 40
KV_HEADS = 8
HEAD_DIM = 128
DEC = 128
RANK = 16


PRIME = 46337
SIGMA_SCALE = 0.3
NEG_LARGE = -1e30
TILE = (8, 128)
SEND_PARTS = 2


def noise_rows(seed_value, matrix_id, positions):
    rank_ids = jnp.arange(RANK, dtype=jnp.int32)
    mixing = (
        seed_value + (matrix_id * RANK + rank_ids)[:, None] * 2749 + positions[None, :] * 6271
    ) % PRIME
    hashed = (mixing * mixing + 1013) % PRIME
    hashed = (hashed * hashed + mixing) % PRIME
    hashed = (hashed * hashed + 1013) % PRIME
    return ((hashed.astype(jnp.float32) * (2.0 / PRIME) - 1.0) * math.sqrt(3.0)).astype(
        jnp.bfloat16
    )


def normed(states, gain):
    values = states.astype(jnp.float32)
    scale = lax.rsqrt(jnp.mean(values * values, axis=-1, keepdims=True) + 1e-06)
    return (values * scale * gain.astype(jnp.float32)).astype(jnp.bfloat16)


def parts_of(values, count):
    parts = []
    for _ in range(count):
        part = lax.reduce_precision(values, 8, 7)
        parts.append(part.astype(jnp.bfloat16))
        values = values - part
    return parts


def expand(inner, rows_b):
    parts = parts_of(inner, 3)
    return jnp.dot(
        jnp.concatenate(parts, axis=1),
        jnp.concatenate([rows_b] * 3, axis=0),
        preferred_element_type=jnp.float32,
    )


def times_rows(left, rows):
    return lax.dot_general(
        left, rows, (((1,), (1,)), ((), ())), preferred_element_type=jnp.float32
    )


def attend(query, keys, values, group, head_dim, prompt_len):
    count = query.shape[0]
    kv_count = keys.shape[1] // head_dim
    query_four = query.reshape(count, kv_count, group, head_dim)
    keys_three = keys.reshape(-1, kv_count, head_dim)
    values_three = values.reshape(-1, kv_count, head_dim)
    scores = jnp.einsum(
        "pkgd,nkd->kgpn", query_four, keys_three, preferred_element_type=jnp.float32
    ) / math.sqrt(head_dim)
    key_index = jnp.arange(keys_three.shape[0], dtype=jnp.int32) - prompt_len
    query_index = jnp.arange(count, dtype=jnp.int32)
    allowed = key_index[None, :] <= query_index[:, None]
    scores = jnp.where(allowed, scores, NEG_LARGE)
    top = jnp.max(scores, axis=-1, keepdims=True)
    exponent = jnp.exp(scores - top)
    weights = (exponent / jnp.sum(exponent, axis=-1, keepdims=True)).astype(jnp.bfloat16)
    mixed = jnp.einsum("kgpn,nkd->pkgd", weights, values_three, preferred_element_type=jnp.float32)
    return mixed.astype(jnp.bfloat16).reshape(count, kv_count * group * head_dim)


def swap_tensor(values):
    return lax.ppermute(values, "tensor", [(0, 1), (1, 0)])


def sum_kernel(steps, own_ref, total_ref, held, landed, send_sems, recv_sems):
    partners = []
    for axis, bit in steps:
        index = lax.axis_index(axis)
        partners.append({axis: index + bit * (1 - 2 * ((index // bit) % 2))})
    barrier = pltpu.get_barrier_semaphore()
    for partner in partners:
        pl.semaphore_signal(
            barrier, inc=1, device_id=partner, device_id_type=pl.DeviceIdType.MESH
        )
    pl.semaphore_wait(barrier, len(steps))
    held[0] = own_ref[...]
    for step, partner in enumerate(partners):
        copy = pltpu.make_async_remote_copy(
            src_ref=held.at[step],
            dst_ref=landed.at[step],
            send_sem=send_sems.at[step],
            recv_sem=recv_sems.at[step],
            device_id=partner,
            device_id_type=pl.DeviceIdType.MESH,
        )
        copy.start()
        copy.wait()
        held[step + 1] = held[step] + landed[step]
    total_ref[...] = held[len(steps)]


def sum_all(tile, members, tensors):
    steps = []
    for axis, size in (("tensor", tensors), ("member", members)):
        bit = 1
        while bit < size:
            steps.append((axis, bit))
            bit *= 2
    count = len(steps)
    return pl.pallas_call(
        functools.partial(sum_kernel, steps),
        out_shape=jax.ShapeDtypeStruct(TILE, jnp.float32),
        in_specs=[pl.BlockSpec(memory_space=pltpu.VMEM)],
        out_specs=pl.BlockSpec(memory_space=pltpu.VMEM),
        scratch_shapes=[
            pltpu.VMEM((count + 1,) + TILE, jnp.float32),
            pltpu.VMEM((count,) + TILE, jnp.float32),
            pltpu.SemaphoreType.DMA((count,)),
            pltpu.SemaphoreType.DMA((count,)),
        ],
        compiler_params=pltpu.CompilerParams(collective_id=0, has_side_effects=True),
    )(tile)


def per_device(
    prompt_states,
    decode_states,
    norm_gain,
    query_bias,
    value_bias,
    w_query,
    w_key,
    w_value,
    w_out,
    targets,
    lengths,
    seeds,
):
    members = lax.axis_size("member")
    tensors = lax.axis_size("tensor")
    member_id = lax.axis_index("member")
    tensor_id = lax.axis_index("tensor")
    shard_width = prompt_states.shape[1]
    prompt_len = prompt_states.shape[0]
    query_width = w_query.shape[1]
    pair_width = w_key.shape[1]
    piece_rows = w_query.shape[0]
    out_piece = w_out.shape[1]
    group = HEADS // KV_HEADS
    sigma = SIGMA_SCALE / math.sqrt(D)
    lift = sigma / math.sqrt(RANK)
    seed_value = seeds[member_id]
    length_plus = lengths[2 * member_id]
    negative_length = lengths[2 * member_id + 1]
    local_rows = jnp.arange(2 * DEC, dtype=jnp.int32)
    plus_rows = local_rows < DEC
    positions = local_rows % DEC
    row_live = positions < jnp.where(plus_rows, length_plus, negative_length)
    column_signs = jnp.where(plus_rows, 1.0, -1.0).astype(jnp.float32)[:, None]

    states = jnp.concatenate([decode_states, prompt_states], axis=0)
    if tensors == 2:
        on_left = tensor_id == 0

        def full_of(own):
            other = swap_tensor(own)
            return jnp.concatenate(
                [jnp.where(on_left, own, other), jnp.where(on_left, other, own)], axis=-1
            )

        states_full, gain_row = full_of(states), full_of(norm_gain)
    else:
        states_full = lax.all_gather(states, "tensor", axis=1, tiled=True)
        gain_row = lax.all_gather(norm_gain, "tensor", axis=0, tiled=True)
    in_all = lax.all_gather(
        jnp.concatenate([w_query, w_key, w_value], axis=1), "member", axis=0, tiled=True
    )
    all_normed = normed(states_full, gain_row)
    row_ids = jnp.arange(D, dtype=jnp.int32)
    query_cols = tensor_id * query_width + jnp.arange(query_width, dtype=jnp.int32)
    pair_cols = tensor_id * pair_width + jnp.arange(pair_width, dtype=jnp.int32)
    tables_left = jnp.concatenate([noise_rows(seed_value, g, row_ids) for g in range(3)], axis=0)
    inner = times_rows(all_normed, tables_left)
    low_query = expand(inner[: 2 * DEC, :RANK], noise_rows(seed_value, 4, query_cols))
    low_key = expand(inner[:, RANK : 2 * RANK], noise_rows(seed_value, 5, pair_cols))
    low_value = expand(inner[:, 2 * RANK :], noise_rows(seed_value, 6, pair_cols))
    low_pair = jnp.concatenate([low_key, low_value], axis=1)
    rows_out = noise_rows(seed_value, 3, query_cols)
    rows_end = noise_rows(seed_value, 7, row_ids)
    w_out, in_all, all_normed, low_query, low_pair, rows_out, rows_end = lax.optimization_barrier(
        (w_out, in_all, all_normed, low_query, low_pair, rows_out, rows_end)
    )
    decode_normed = all_normed[: 2 * DEC]
    query_all, pair_all = in_all[:, :query_width], in_all[:, query_width:]
    out_all = lax.all_gather(w_out.T, "member", axis=0, tiled=True)
    pair_bias = jnp.concatenate(
        [jnp.zeros((pair_width,), jnp.float32), value_bias.astype(jnp.float32)]
    )
    query_base = jnp.dot(decode_normed, query_all, preferred_element_type=jnp.float32)
    pair_base = jnp.dot(all_normed, pair_all, preferred_element_type=jnp.float32)
    query = (query_base + query_bias.astype(jnp.float32) + column_signs * lift * low_query).astype(
        jnp.bfloat16
    )
    pair_base = pair_base + pair_bias
    mixed_parts = []
    for sign_index in range(2):
        sign = 1.0 - 2.0 * sign_index
        first = sign_index * DEC
        last = first + DEC
        own = jnp.concatenate([pair_base[2 * DEC :], pair_base[first:last]], axis=0)
        own_low = jnp.concatenate([low_pair[2 * DEC :], low_pair[first:last]], axis=0)
        pair = (own + sign * lift * own_low).astype(jnp.bfloat16)
        mixed_parts.append(
            attend(
                query[first:last],
                pair[:, :pair_width],
                pair[:, pair_width:],
                group,
                HEAD_DIM,
                prompt_len,
            )
        )
    mixed = jnp.concatenate(mixed_parts, axis=0)
    out_inner = times_rows(mixed, rows_out)
    out_low = expand(out_inner, rows_end)
    out_low = column_signs * lift * out_low


    def partial_of(first, count):
        weights = lax.dynamic_slice_in_dim(out_all, first, count, 0)
        low = lax.dynamic_slice_in_dim(out_low, first, count, 1)
        return (times_rows(mixed, weights) + low).astype(jnp.bfloat16)

    fitness_errors = jnp.zeros((2 * DEC,), jnp.float32)
    if tensors == 2:
        width = shard_width // SEND_PARTS
        received = []
        for part in range(SEND_PARTS):
            away = partial_of((1 - tensor_id) * shard_width + part * width, width)
            received.append(swap_tensor(away))
        for part in range(SEND_PARTS):
            own = partial_of(tensor_id * shard_width + part * width, width)
            summed = own.astype(jnp.float32) + received[part].astype(jnp.float32)
            goal = targets[:, part * width : (part + 1) * width]
            difference = summed - goal.astype(jnp.float32)
            fitness_errors = fitness_errors + jnp.sum(difference * difference, axis=1)
    else:
        summed = lax.psum(partial_of(0, D), "tensor").astype(jnp.float32)
        summed = lax.dynamic_slice_in_dim(summed, tensor_id * shard_width, shard_width, 1)
        difference = summed - targets.astype(jnp.float32)
        fitness_errors = jnp.sum(difference * difference, axis=1)
    fitness_errors = fitness_errors / D
    fitness_errors = jnp.where(row_live, fitness_errors, 0.0)
    pair_total = jnp.stack(
        [
            jnp.sum(fitness_errors[:DEC]) / length_plus.astype(jnp.float32),
            jnp.sum(fitness_errors[DEC:]) / negative_length.astype(jnp.float32),
        ]
    )
    spread = lax.dynamic_update_slice_in_dim(
        jnp.zeros((TILE[1],), jnp.float32), pair_total, 2 * member_id, 0
    )
    spread = jnp.zeros(TILE, jnp.float32).at[0].set(spread)
    fitness = -sum_all(spread, members, tensors)[0, : 2 * members]
    differences = fitness[0::2] - fitness[1::2]
    factor = 1.0 / (2.0 * members * sigma * math.sqrt(RANK))
    row_of_weights = differences * factor
    own_rows = member_id * piece_rows + jnp.arange(piece_rows, dtype=jnp.int32)
    own_out_cols = member_id * out_piece + jnp.arange(out_piece, dtype=jnp.int32)

    def all_rows(matrix_id, ids):
        tables = jax.vmap(lambda seed_one: noise_rows(seed_one, matrix_id, ids))(seeds)
        return tables.reshape(members * RANK, ids.shape[0])

    row_weights = jnp.repeat(row_of_weights, RANK)[:, None]

    def update(first_id, second_id, left_ids, right_ids):
        left = all_rows(first_id, left_ids)
        right = all_rows(second_id, right_ids)
        if left_ids.shape[0] <= right_ids.shape[0]:
            left = jnp.concatenate(parts_of(left.astype(jnp.float32) * row_weights, 2), axis=0)
            right = jnp.concatenate([right, right], axis=0)
        else:
            right = jnp.concatenate(parts_of(right.astype(jnp.float32) * row_weights, 2), axis=0)
            left = jnp.concatenate([left, left], axis=0)
        return lax.dot_general(
            left, right, (((0,), (0,)), ((), ())), preferred_element_type=jnp.float32
        )

    grad_query = update(0, 4, own_rows, query_cols)
    grad_key = update(1, 5, own_rows, pair_cols)
    grad_value = update(2, 6, own_rows, pair_cols)
    grad_out = update(3, 7, query_cols, own_out_cols)
    return (fitness, grad_query, grad_key, grad_value, grad_out)


def solution(mesh):
    placed = (
        P("member", "tensor"),
        P("member", "tensor"),
        P("tensor"),
        P("tensor"),
        P("tensor"),
        P("member", "tensor"),
        P("member", "tensor"),
        P("member", "tensor"),
        P("tensor", "member"),
        P("member", "tensor"),
        P(),
        P(),
    )
    return jax.shard_map(
        per_device,
        mesh=mesh,
        in_specs=placed,
        out_specs=(
            P(),
            P("member", "tensor"),
            P("member", "tensor"),
            P("member", "tensor"),
            P("tensor", "member"),
        ),
        check_vma=False,
    )
```

```python
import functools
import math

import jax
import jax.numpy as jnp
from jax import lax
from jax.experimental import pallas as pl
from jax.experimental.pallas import tpu as pltpu
from jax.sharding import PartitionSpec as P

D = 5120
HEADS = 40
KV_HEADS = 8
HEAD_DIM = 128
DEC = 128
RANK = 16


PRIME = 46337
SIGMA_SCALE = 0.3
NEG_LARGE = -1e30
TILE = (8, 128)


def noise_rows(seed_value, matrix_id, positions):
    rank_ids = jnp.arange(RANK, dtype=jnp.int32)
    mixing = (
        seed_value + (matrix_id * RANK + rank_ids)[:, None] * 2749 + positions[None, :] * 6271
    ) % PRIME
    hashed = (mixing * mixing + 1013) % PRIME
    hashed = (hashed * hashed + mixing) % PRIME
    hashed = (hashed * hashed + 1013) % PRIME
    return ((hashed.astype(jnp.float32) * (2.0 / PRIME) - 1.0) * math.sqrt(3.0)).astype(
        jnp.bfloat16
    )


def normed(states, gain):
    values = states.astype(jnp.float32)
    scale = lax.rsqrt(jnp.mean(values * values, axis=-1, keepdims=True) + 1e-06)
    return (values * scale * gain.astype(jnp.float32)).astype(jnp.bfloat16)


def parts_of(values, count):
    parts = []
    for _ in range(count):
        part = lax.reduce_precision(values, 8, 7)
        parts.append(part.astype(jnp.bfloat16))
        values = values - part
    return parts


def expand(inner, rows_b):
    parts = parts_of(inner, 3)
    return jnp.dot(
        jnp.concatenate(parts, axis=1),
        jnp.concatenate([rows_b] * 3, axis=0),
        preferred_element_type=jnp.float32,
    )


def times_rows(left, rows):
    return lax.dot_general(
        left, rows, (((1,), (1,)), ((), ())), preferred_element_type=jnp.float32
    )


def attend(query, keys, values, group, head_dim, prompt_len):
    count = query.shape[0]
    kv_count = keys.shape[1] // head_dim
    query_four = query.reshape(count, kv_count, group, head_dim)
    keys_three = keys.reshape(-1, kv_count, head_dim)
    values_three = values.reshape(-1, kv_count, head_dim)
    scores = jnp.einsum(
        "pkgd,nkd->kgpn", query_four, keys_three, preferred_element_type=jnp.float32
    ) / math.sqrt(head_dim)
    key_index = jnp.arange(keys_three.shape[0], dtype=jnp.int32) - prompt_len
    query_index = jnp.arange(count, dtype=jnp.int32)
    allowed = key_index[None, :] <= query_index[:, None]
    scores = jnp.where(allowed, scores, NEG_LARGE)
    top = jnp.max(scores, axis=-1, keepdims=True)
    exponent = jnp.exp(scores - top)
    weights = (exponent / jnp.sum(exponent, axis=-1, keepdims=True)).astype(jnp.bfloat16)
    mixed = jnp.einsum("kgpn,nkd->pkgd", weights, values_three, preferred_element_type=jnp.float32)
    return mixed.astype(jnp.bfloat16).reshape(count, kv_count * group * head_dim)


def swap_tensor(values):
    return lax.ppermute(values, "tensor", [(0, 1), (1, 0)])


def sum_kernel(steps, own_ref, total_ref, held, landed, send_sems, recv_sems):
    partners = []
    for axis, bit in steps:
        index = lax.axis_index(axis)
        partners.append({axis: index + bit * (1 - 2 * ((index // bit) % 2))})
    barrier = pltpu.get_barrier_semaphore()
    for partner in partners:
        pl.semaphore_signal(
            barrier, inc=1, device_id=partner, device_id_type=pl.DeviceIdType.MESH
        )
    pl.semaphore_wait(barrier, len(steps))
    held[0] = own_ref[...]
    for step, partner in enumerate(partners):
        copy = pltpu.make_async_remote_copy(
            src_ref=held.at[step],
            dst_ref=landed.at[step],
            send_sem=send_sems.at[step],
            recv_sem=recv_sems.at[step],
            device_id=partner,
            device_id_type=pl.DeviceIdType.MESH,
        )
        copy.start()
        copy.wait()
        held[step + 1] = held[step] + landed[step]
    total_ref[...] = held[len(steps)]


def sum_all(tile, members, tensors):
    steps = []
    for axis, size in (("tensor", tensors), ("member", members)):
        bit = 1
        while bit < size:
            steps.append((axis, bit))
            bit *= 2
    count = len(steps)
    return pl.pallas_call(
        functools.partial(sum_kernel, steps),
        out_shape=jax.ShapeDtypeStruct(TILE, jnp.float32),
        in_specs=[pl.BlockSpec(memory_space=pltpu.VMEM)],
        out_specs=pl.BlockSpec(memory_space=pltpu.VMEM),
        scratch_shapes=[
            pltpu.VMEM((count + 1,) + TILE, jnp.float32),
            pltpu.VMEM((count,) + TILE, jnp.float32),
            pltpu.SemaphoreType.DMA((count,)),
            pltpu.SemaphoreType.DMA((count,)),
        ],
        compiler_params=pltpu.CompilerParams(collective_id=0, has_side_effects=True),
    )(tile)


def per_device(
    prompt_states,
    decode_states,
    norm_gain,
    query_bias,
    value_bias,
    w_query,
    w_key,
    w_value,
    w_out,
    targets,
    lengths,
    seeds,
):
    members = lax.axis_size("member")
    tensors = lax.axis_size("tensor")
    member_id = lax.axis_index("member")
    tensor_id = lax.axis_index("tensor")
    shard_width = prompt_states.shape[1]
    prompt_len = prompt_states.shape[0]
    query_width = w_query.shape[1]
    pair_width = w_key.shape[1]
    piece_rows = w_query.shape[0]
    out_piece = w_out.shape[1]
    group = HEADS // KV_HEADS
    sigma = SIGMA_SCALE / math.sqrt(D)
    lift = sigma / math.sqrt(RANK)
    seed_value = seeds[member_id]
    length_plus = lengths[2 * member_id]
    negative_length = lengths[2 * member_id + 1]
    local_rows = jnp.arange(2 * DEC, dtype=jnp.int32)
    plus_rows = local_rows < DEC
    positions = local_rows % DEC
    row_live = positions < jnp.where(plus_rows, length_plus, negative_length)
    column_signs = jnp.where(plus_rows, 1.0, -1.0).astype(jnp.float32)[:, None]

    states = jnp.concatenate([decode_states, prompt_states], axis=0)
    if tensors == 2:
        on_left = tensor_id == 0

        def full_of(own):
            other = swap_tensor(own)
            return jnp.concatenate(
                [jnp.where(on_left, own, other), jnp.where(on_left, other, own)], axis=-1
            )

        states_full, gain_row = full_of(states), full_of(norm_gain)
    else:
        states_full = lax.all_gather(states, "tensor", axis=1, tiled=True)
        gain_row = lax.all_gather(norm_gain, "tensor", axis=0, tiled=True)
    fold = members // tensors
    moves = []
    for member in range(members):
        for tensor in range(tensors):
            target = (tensor * fold + member % fold) * tensors + member // fold
            if target != member * tensors + tensor:
                moves.append((member * tensors + tensor, target))
    out_own = w_out.T
    out_moved = lax.ppermute(out_own, ("member", "tensor"), moves)
    out_own = jnp.where(member_id // fold == tensor_id, out_own, out_moved)
    in_all = lax.all_gather(
        jnp.concatenate([w_query, w_key, w_value], axis=1), "member", axis=0, tiled=True
    )
    all_normed = normed(states_full, gain_row)
    row_ids = jnp.arange(D, dtype=jnp.int32)
    query_cols = tensor_id * query_width + jnp.arange(query_width, dtype=jnp.int32)
    pair_cols = tensor_id * pair_width + jnp.arange(pair_width, dtype=jnp.int32)
    tables_left = jnp.concatenate([noise_rows(seed_value, g, row_ids) for g in range(3)], axis=0)
    inner = times_rows(all_normed, tables_left)
    low_query = expand(inner[: 2 * DEC, :RANK], noise_rows(seed_value, 4, query_cols))
    low_key = expand(inner[:, RANK : 2 * RANK], noise_rows(seed_value, 5, pair_cols))
    low_value = expand(inner[:, 2 * RANK :], noise_rows(seed_value, 6, pair_cols))
    low_pair = jnp.concatenate([low_key, low_value], axis=1)
    rows_out = noise_rows(seed_value, 3, row_ids)
    rows_end = noise_rows(
        seed_value, 7, tensor_id * shard_width + jnp.arange(shard_width, dtype=jnp.int32)
    )
    out_own, in_all, all_normed, low_query, low_pair, rows_out, rows_end = lax.optimization_barrier(
        (out_own, in_all, all_normed, low_query, low_pair, rows_out, rows_end)
    )
    decode_normed = all_normed[: 2 * DEC]
    query_all, pair_all = in_all[:, :query_width], in_all[:, query_width:]
    out_all = lax.all_gather(out_own, "member", axis=0, tiled=True)
    pair_bias = jnp.concatenate(
        [jnp.zeros((pair_width,), jnp.float32), value_bias.astype(jnp.float32)]
    )
    query_base = jnp.dot(decode_normed, query_all, preferred_element_type=jnp.float32)
    pair_base = jnp.dot(all_normed, pair_all, preferred_element_type=jnp.float32)
    query = (query_base + query_bias.astype(jnp.float32) + column_signs * lift * low_query).astype(
        jnp.bfloat16
    )
    pair_base = pair_base + pair_bias
    mixed_parts = []
    for sign_index in range(2):
        sign = 1.0 - 2.0 * sign_index
        first = sign_index * DEC
        last = first + DEC
        own = jnp.concatenate([pair_base[2 * DEC :], pair_base[first:last]], axis=0)
        own_low = jnp.concatenate([low_pair[2 * DEC :], low_pair[first:last]], axis=0)
        pair = (own + sign * lift * own_low).astype(jnp.bfloat16)
        mixed = attend(
            query[first:last],
            pair[:, :pair_width],
            pair[:, pair_width:],
            group,
            HEAD_DIM,
            prompt_len,
        )
        mixed_parts.append(
            full_of(mixed)
            if tensors == 2
            else lax.all_gather(mixed, "tensor", axis=1, tiled=True)
        )
    mixed = jnp.concatenate(mixed_parts, axis=0)

    lows = []
    for share in range(tensors):
        heads = slice(share * query_width, (share + 1) * query_width)
        low = expand(times_rows(mixed[:, heads], rows_out[:, heads]), rows_end)
        lows.append(column_signs * lift * low)
    summed = jnp.zeros((2 * DEC, shard_width), jnp.float32)
    for share in range(tensors):
        heads = slice(share * query_width, (share + 1) * query_width)
        weights = out_all[share * shard_width : (share + 1) * shard_width]
        partial = (times_rows(mixed[:, heads], weights) + lows[share]).astype(jnp.bfloat16)
        summed = summed + partial.astype(jnp.float32)
    difference = summed - targets.astype(jnp.float32)
    fitness_errors = jnp.sum(difference * difference, axis=1)
    fitness_errors = fitness_errors / D
    fitness_errors = jnp.where(row_live, fitness_errors, 0.0)
    pair_total = jnp.stack(
        [
            jnp.sum(fitness_errors[:DEC]) / length_plus.astype(jnp.float32),
            jnp.sum(fitness_errors[DEC:]) / negative_length.astype(jnp.float32),
        ]
    )
    spread = lax.dynamic_update_slice_in_dim(
        jnp.zeros((TILE[1],), jnp.float32), pair_total, 2 * member_id, 0
    )
    spread = jnp.zeros(TILE, jnp.float32).at[0].set(spread)
    fitness = -sum_all(spread, members, tensors)[0, : 2 * members]
    differences = fitness[0::2] - fitness[1::2]
    factor = 1.0 / (2.0 * members * sigma * math.sqrt(RANK))
    row_of_weights = differences * factor
    own_rows = member_id * piece_rows + jnp.arange(piece_rows, dtype=jnp.int32)
    own_out_cols = member_id * out_piece + jnp.arange(out_piece, dtype=jnp.int32)

    def all_rows(matrix_id, ids):
        tables = jax.vmap(lambda seed_one: noise_rows(seed_one, matrix_id, ids))(seeds)
        return tables.reshape(members * RANK, ids.shape[0])

    row_weights = jnp.repeat(row_of_weights, RANK)[:, None]

    def update(first_id, second_id, left_ids, right_ids):
        left = all_rows(first_id, left_ids)
        right = all_rows(second_id, right_ids)
        if left_ids.shape[0] <= right_ids.shape[0]:
            left = jnp.concatenate(parts_of(left.astype(jnp.float32) * row_weights, 2), axis=0)
            right = jnp.concatenate([right, right], axis=0)
        else:
            right = jnp.concatenate(parts_of(right.astype(jnp.float32) * row_weights, 2), axis=0)
            left = jnp.concatenate([left, left], axis=0)
        return lax.dot_general(
            left, right, (((0,), (0,)), ((), ())), preferred_element_type=jnp.float32
        )

    grad_query = update(0, 4, own_rows, query_cols)
    grad_key = update(1, 5, own_rows, pair_cols)
    grad_value = update(2, 6, own_rows, pair_cols)
    grad_out = update(3, 7, query_cols, own_out_cols)
    return (fitness, grad_query, grad_key, grad_value, grad_out)


def solution(mesh):
    placed = (
        P("member", "tensor"),
        P("member", "tensor"),
        P("tensor"),
        P("tensor"),
        P("tensor"),
        P("member", "tensor"),
        P("member", "tensor"),
        P("member", "tensor"),
        P("tensor", "member"),
        P("member", "tensor"),
        P(),
        P(),
    )
    return jax.shard_map(
        per_device,
        mesh=mesh,
        in_specs=placed,
        out_specs=(
            P(),
            P("member", "tensor"),
            P("member", "tensor"),
            P("member", "tensor"),
            P("tensor", "member"),
        ),
        check_vma=False,
    )
```

```python
import functools
import math

import jax
import jax.numpy as jnp
from jax import lax
from jax.experimental import pallas as pl
from jax.experimental.pallas import tpu as pltpu
from jax.sharding import PartitionSpec as P

D = 5120
HEADS = 40
KV_HEADS = 8
HEAD_DIM = 128
DEC = 128
RANK = 16


PRIME = 46337
SIGMA_SCALE = 0.3
NEG_LARGE = -1e30
TILE = (8, 128)
SEND_PARTS = 2


def noise_rows(seed_value, matrix_id, positions):
    rank_ids = jnp.arange(RANK, dtype=jnp.int32)
    mixing = (
        seed_value + (matrix_id * RANK + rank_ids)[:, None] * 2749 + positions[None, :] * 6271
    ) % PRIME
    hashed = (mixing * mixing + 1013) % PRIME
    hashed = (hashed * hashed + mixing) % PRIME
    hashed = (hashed * hashed + 1013) % PRIME
    return ((hashed.astype(jnp.float32) * (2.0 / PRIME) - 1.0) * math.sqrt(3.0)).astype(
        jnp.bfloat16
    )


def normed(states, gain):
    values = states.astype(jnp.float32)
    scale = lax.rsqrt(jnp.mean(values * values, axis=-1, keepdims=True) + 1e-06)
    return (values * scale * gain.astype(jnp.float32)).astype(jnp.bfloat16)


def parts_of(values, count):
    parts = []
    for _ in range(count):
        part = lax.reduce_precision(values, 8, 7)
        parts.append(part.astype(jnp.bfloat16))
        values = values - part
    return parts


def expand(inner, rows_b):
    parts = parts_of(inner, 3)
    return jnp.dot(
        jnp.concatenate(parts, axis=1),
        jnp.concatenate([rows_b] * 3, axis=0),
        preferred_element_type=jnp.float32,
    )


def times_rows(left, rows):
    return lax.dot_general(
        left, rows, (((1,), (1,)), ((), ())), preferred_element_type=jnp.float32
    )


def attend(query, keys, values, group, head_dim, prompt_len):
    count = query.shape[0]
    kv_count = keys.shape[1] // head_dim
    query_four = query.reshape(count, kv_count, group, head_dim)
    keys_three = keys.reshape(-1, kv_count, head_dim)
    values_three = values.reshape(-1, kv_count, head_dim)
    scores = jnp.einsum(
        "pkgd,nkd->kgpn", query_four, keys_three, preferred_element_type=jnp.float32
    ) / math.sqrt(head_dim)
    key_index = jnp.arange(keys_three.shape[0], dtype=jnp.int32) - prompt_len
    query_index = jnp.arange(count, dtype=jnp.int32)
    allowed = key_index[None, :] <= query_index[:, None]
    scores = jnp.where(allowed, scores, NEG_LARGE)
    top = jnp.max(scores, axis=-1, keepdims=True)
    exponent = jnp.exp(scores - top)
    weights = (exponent / jnp.sum(exponent, axis=-1, keepdims=True)).astype(jnp.bfloat16)
    mixed = jnp.einsum("kgpn,nkd->pkgd", weights, values_three, preferred_element_type=jnp.float32)
    return mixed.astype(jnp.bfloat16).reshape(count, kv_count * group * head_dim)


def swap_tensor(values):
    return lax.ppermute(values, "tensor", [(0, 1), (1, 0)])


def sum_kernel(steps, own_ref, total_ref, held, landed, send_sems, recv_sems):
    partners = []
    for axis, bit in steps:
        index = lax.axis_index(axis)
        partners.append({axis: index + bit * (1 - 2 * ((index // bit) % 2))})
    barrier = pltpu.get_barrier_semaphore()
    for partner in partners:
        pl.semaphore_signal(
            barrier, inc=1, device_id=partner, device_id_type=pl.DeviceIdType.MESH
        )
    pl.semaphore_wait(barrier, len(steps))
    held[0] = own_ref[...]
    for step, partner in enumerate(partners):
        copy = pltpu.make_async_remote_copy(
            src_ref=held.at[step],
            dst_ref=landed.at[step],
            send_sem=send_sems.at[step],
            recv_sem=recv_sems.at[step],
            device_id=partner,
            device_id_type=pl.DeviceIdType.MESH,
        )
        copy.start()
        copy.wait()
        held[step + 1] = held[step] + landed[step]
    total_ref[...] = held[len(steps)]


def sum_all(tile, members, tensors):
    steps = []
    for axis, size in (("tensor", tensors), ("member", members)):
        bit = 1
        while bit < size:
            steps.append((axis, bit))
            bit *= 2
    count = len(steps)
    return pl.pallas_call(
        functools.partial(sum_kernel, steps),
        out_shape=jax.ShapeDtypeStruct(TILE, jnp.float32),
        in_specs=[pl.BlockSpec(memory_space=pltpu.VMEM)],
        out_specs=pl.BlockSpec(memory_space=pltpu.VMEM),
        scratch_shapes=[
            pltpu.VMEM((count + 1,) + TILE, jnp.float32),
            pltpu.VMEM((count,) + TILE, jnp.float32),
            pltpu.SemaphoreType.DMA((count,)),
            pltpu.SemaphoreType.DMA((count,)),
        ],
        compiler_params=pltpu.CompilerParams(collective_id=0, has_side_effects=True),
    )(tile)


def per_device(
    prompt_states,
    decode_states,
    norm_gain,
    query_bias,
    value_bias,
    w_query,
    w_key,
    w_value,
    w_out,
    targets,
    lengths,
    seeds,
):
    members = lax.axis_size("member")
    tensors = lax.axis_size("tensor")
    member_id = lax.axis_index("member")
    tensor_id = lax.axis_index("tensor")
    shard_width = prompt_states.shape[1]
    prompt_len = prompt_states.shape[0]
    query_width = w_query.shape[1]
    pair_width = w_key.shape[1]
    piece_rows = w_query.shape[0]
    out_piece = w_out.shape[1]
    group = HEADS // KV_HEADS
    sigma = SIGMA_SCALE / math.sqrt(D)
    lift = sigma / math.sqrt(RANK)
    seed_value = seeds[member_id]
    length_plus = lengths[2 * member_id]
    negative_length = lengths[2 * member_id + 1]
    local_rows = jnp.arange(2 * DEC, dtype=jnp.int32)
    plus_rows = local_rows < DEC
    positions = local_rows % DEC
    row_live = positions < jnp.where(plus_rows, length_plus, negative_length)
    column_signs = jnp.where(plus_rows, 1.0, -1.0).astype(jnp.float32)[:, None]

    states = jnp.concatenate([decode_states, prompt_states], axis=0)
    if tensors == 2:
        on_left = tensor_id == 0

        def full_of(own):
            other = swap_tensor(own)
            return jnp.concatenate(
                [jnp.where(on_left, own, other), jnp.where(on_left, other, own)], axis=-1
            )

        states_full, gain_row = full_of(states), full_of(norm_gain)
    else:
        states_full = lax.all_gather(states, "tensor", axis=1, tiled=True)
        gain_row = lax.all_gather(norm_gain, "tensor", axis=0, tiled=True)
    in_all = lax.all_gather(
        jnp.concatenate([w_query, w_key, w_value], axis=1), "member", axis=0, tiled=True
    )
    all_normed = normed(states_full, gain_row)
    row_ids = jnp.arange(D, dtype=jnp.int32)
    query_cols = tensor_id * query_width + jnp.arange(query_width, dtype=jnp.int32)
    pair_cols = tensor_id * pair_width + jnp.arange(pair_width, dtype=jnp.int32)
    tables_left = jnp.concatenate([noise_rows(seed_value, g, row_ids) for g in range(3)], axis=0)
    inner = times_rows(all_normed, tables_left)
    low_query = expand(inner[: 2 * DEC, :RANK], noise_rows(seed_value, 4, query_cols))
    low_key = expand(inner[:, RANK : 2 * RANK], noise_rows(seed_value, 5, pair_cols))
    low_value = expand(inner[:, 2 * RANK :], noise_rows(seed_value, 6, pair_cols))
    low_pair = jnp.concatenate([low_key, low_value], axis=1)
    rows_out = noise_rows(seed_value, 3, query_cols)
    rows_end = noise_rows(seed_value, 7, row_ids)
    w_out, in_all, all_normed, low_query, low_pair, rows_out, rows_end = lax.optimization_barrier(
        (w_out, in_all, all_normed, low_query, low_pair, rows_out, rows_end)
    )
    decode_normed = all_normed[: 2 * DEC]
    query_all, pair_all = in_all[:, :query_width], in_all[:, query_width:]
    out_all = lax.all_gather(w_out.T, "member", axis=0, tiled=True)
    pair_bias = jnp.concatenate(
        [jnp.zeros((pair_width,), jnp.float32), value_bias.astype(jnp.float32)]
    )
    query_base = jnp.dot(decode_normed, query_all, preferred_element_type=jnp.float32)
    pair_base = jnp.dot(all_normed, pair_all, preferred_element_type=jnp.float32)
    query = (query_base + query_bias.astype(jnp.float32) + column_signs * lift * low_query).astype(
        jnp.bfloat16
    )
    pair_base = pair_base + pair_bias
    mixed_parts = []
    for sign_index in range(2):
        sign = 1.0 - 2.0 * sign_index
        first = sign_index * DEC
        last = first + DEC
        own = jnp.concatenate([pair_base[2 * DEC :], pair_base[first:last]], axis=0)
        own_low = jnp.concatenate([low_pair[2 * DEC :], low_pair[first:last]], axis=0)
        pair = (own + sign * lift * own_low).astype(jnp.bfloat16)
        mixed_parts.append(
            attend(
                query[first:last],
                pair[:, :pair_width],
                pair[:, pair_width:],
                group,
                HEAD_DIM,
                prompt_len,
            )
        )
    mixed = jnp.concatenate(mixed_parts, axis=0)
    out_inner = times_rows(mixed, rows_out)
    out_low = expand(out_inner, rows_end)
    out_low = column_signs * lift * out_low


    def partial_of(first, count):
        weights = lax.dynamic_slice_in_dim(out_all, first, count, 0)
        low = lax.dynamic_slice_in_dim(out_low, first, count, 1)
        return (times_rows(mixed, weights) + low).astype(jnp.bfloat16)

    fitness_errors = jnp.zeros((2 * DEC,), jnp.float32)
    if tensors == 2:
        width = shard_width // SEND_PARTS
        received = []
        for part in range(SEND_PARTS):
            away = partial_of((1 - tensor_id) * shard_width + part * width, width)
            received.append(swap_tensor(away))
        owns = lax.optimization_barrier(
            [
                partial_of(tensor_id * shard_width + part * width, width)
                for part in range(SEND_PARTS)
            ]
        )
        for part in range(SEND_PARTS):
            summed = owns[part].astype(jnp.float32) + received[part].astype(jnp.float32)
            goal = targets[:, part * width : (part + 1) * width]
            difference = summed - goal.astype(jnp.float32)
            fitness_errors = fitness_errors + jnp.sum(difference * difference, axis=1)
    else:
        summed = lax.psum(partial_of(0, D), "tensor").astype(jnp.float32)
        summed = lax.dynamic_slice_in_dim(summed, tensor_id * shard_width, shard_width, 1)
        difference = summed - targets.astype(jnp.float32)
        fitness_errors = jnp.sum(difference * difference, axis=1)
    fitness_errors = fitness_errors / D
    fitness_errors = jnp.where(row_live, fitness_errors, 0.0)
    pair_total = jnp.stack(
        [
            jnp.sum(fitness_errors[:DEC]) / length_plus.astype(jnp.float32),
            jnp.sum(fitness_errors[DEC:]) / negative_length.astype(jnp.float32),
        ]
    )
    spread = lax.dynamic_update_slice_in_dim(
        jnp.zeros((TILE[1],), jnp.float32), pair_total, 2 * member_id, 0
    )
    spread = jnp.zeros(TILE, jnp.float32).at[0].set(spread)
    fitness = -sum_all(spread, members, tensors)[0, : 2 * members]
    differences = fitness[0::2] - fitness[1::2]
    factor = 1.0 / (2.0 * members * sigma * math.sqrt(RANK))
    row_of_weights = differences * factor
    own_rows = member_id * piece_rows + jnp.arange(piece_rows, dtype=jnp.int32)
    own_out_cols = member_id * out_piece + jnp.arange(out_piece, dtype=jnp.int32)

    def all_rows(matrix_id, ids):
        tables = jax.vmap(lambda seed_one: noise_rows(seed_one, matrix_id, ids))(seeds)
        return tables.reshape(members * RANK, ids.shape[0])

    row_weights = jnp.repeat(row_of_weights, RANK)[:, None]

    def update(first_id, second_id, left_ids, right_ids):
        left = all_rows(first_id, left_ids)
        right = all_rows(second_id, right_ids)
        if left_ids.shape[0] <= right_ids.shape[0]:
            left = jnp.concatenate(parts_of(left.astype(jnp.float32) * row_weights, 2), axis=0)
            right = jnp.concatenate([right, right], axis=0)
        else:
            right = jnp.concatenate(parts_of(right.astype(jnp.float32) * row_weights, 2), axis=0)
            left = jnp.concatenate([left, left], axis=0)
        return lax.dot_general(
            left, right, (((0,), (0,)), ((), ())), preferred_element_type=jnp.float32
        )

    grad_query = update(0, 4, own_rows, query_cols)
    grad_key = update(1, 5, own_rows, pair_cols)
    grad_value = update(2, 6, own_rows, pair_cols)
    grad_out = update(3, 7, query_cols, own_out_cols)
    return (fitness, grad_query, grad_key, grad_value, grad_out)


def solution(mesh):
    placed = (
        P("member", "tensor"),
        P("member", "tensor"),
        P("tensor"),
        P("tensor"),
        P("tensor"),
        P("member", "tensor"),
        P("member", "tensor"),
        P("member", "tensor"),
        P("tensor", "member"),
        P("member", "tensor"),
        P(),
        P(),
    )
    return jax.shard_map(
        per_device,
        mesh=mesh,
        in_specs=placed,
        out_specs=(
            P(),
            P("member", "tensor"),
            P("member", "tensor"),
            P("member", "tensor"),
            P("tensor", "member"),
        ),
        check_vma=False,
    )
```
